512 devices in a mesh: replica: 8 (over y_lo, x), fsdp: 64 (over y_hi, z, core).
Axes of the slice: x: 4, y: 4 (y_hi: 2, y_lo: 2; y = y_hi * 2 + y_lo), z: 16, core: 2. Of those that a mesh axis runs over, the one named last changes fastest.
Arguments:
- inputs: bfloat16 [8, 8192, 4096], P('replica', 'fsdp'), may hold values from -6 to 6
- upstream: bfloat16 [8, 8192, 512], P('replica', 'fsdp'), may hold values from -6 to 6
- params: float32 [8, 4096, 512], P('replica', 'fsdp'), may hold values from -6 to 6
- first_moment: float32 [8, 4096, 512], P('replica', 'fsdp'), may hold values from -3 to 3
- second_moment: float32 [8, 4096, 512], P('replica', 'fsdp'), may hold values from 0.05 to 1
- anchor: float32 [4096, 512], P('fsdp'), may hold values from -6 to 6
- outer_moment: float32 [4096, 512], P('fsdp'), may hold values from -3 to 3
- step_count: int32 [1], replicated, may hold values from 1 to 8
Outputs:
- new_params: float32 [8, 4096, 512], P('replica', 'fsdp')
- new_first: float32 [8, 4096, 512], P('replica', 'fsdp')
- new_second: float32 [8, 4096, 512], P('replica', 'fsdp')
- new_anchor: float32 [4096, 512], P('fsdp')
- new_outer: float32 [4096, 512], P('fsdp')
- input_grad: bfloat16 [8, 8192, 4096], P('replica', 'fsdp')
The draws below stay inside these ranges and needn't reach their ends.
All inputs are finite; a program needn't handle non-finite values.
Results may differ from the reference program's by a relative error of at most 0.006.
Values may be sent and summed in bfloat16 or wider, within the bound.
No kernel may reach another device: no remote copies, remote signals or barrier semaphores. Data moves between devices by JAX's collectives and lax.ppermute only.
A program may use at most 64 MiB of HBM per device.

```python
import math
import jax
import jax.numpy as jnp
from jax import lax

D = 4096
KV = 512
TOKENS = 8192
REPLICAS = 8


def levels(rng, dims, shards, least, high):
    factor_of = 1.0
    for position, blocks in shards:
        draws = jax.random.uniform(jax.random.fold_in(jax.random.fold_in(rng, 6), position), (blocks,), jnp.float32, least / len(shards), high / len(shards))
        factor_of = factor_of * jnp.repeat(jnp.exp(draws), dims[position] // blocks).reshape((-1,) + (1,) * (len(dims) - 1 - position))
    return factor_of


def normal_values(own_key, dims, width, most, shards=(), held_as=jnp.bfloat16):
    gain = levels(own_key, dims, shards, -0.22, 0.18) if shards else 1.0
    result = jax.random.normal(own_key, dims, jnp.float32) * width * gain
    return jnp.minimum(jnp.maximum(result, -most), most).astype(held_as)


def setup_inputs(seed: int = 0) -> dict:
    streams_of = jax.random.split(jax.random.key(seed), 9)
    return {
        "inputs": normal_values(streams_of[0], (REPLICAS, TOKENS, D), 1.0, 6.0, ((0, 8), (1, 64))),
        "upstream": normal_values(streams_of[1], (REPLICAS, TOKENS, KV), 1.0, 6.0, ((0, 8), (1, 64))),
        "params": normal_values(streams_of[2], (REPLICAS, D, KV), 1.0, 6.0, ((0, 8), (1, 64)), jnp.float32),
        "first_moment": normal_values(streams_of[3], (REPLICAS, D, KV), 0.3, 3.0, ((0, 8), (1, 64)), jnp.float32),
        "second_moment": jnp.clip(jnp.exp(math.log(1.0) - 2.9957323 * jax.random.uniform(streams_of[4], (REPLICAS, D, KV), jnp.float32) ** levels(streams_of[4], (REPLICAS, D, KV), ((0, 8), (1, 64)), -0.2, 0.2)), 0.05, 1.0),
        "anchor": normal_values(streams_of[5], (D, KV), 1.0, 6.0, ((0, 64),), jnp.float32),
        "outer_moment": normal_values(streams_of[6], (D, KV), 0.3, 3.0, ((0, 64),), jnp.float32),
        "step_count": jax.random.randint(streams_of[7], (1,), 1, 9).astype(jnp.int32),
    }


def one_replica(inputs, upstream, params, first_moment, second_moment, anchor, step_count, outer_grad_unused):
    inv_root = 1.0 / jnp.sqrt(jnp.float32(D))
    weight_bf = params.astype(jnp.bfloat16)
    preact = jnp.dot(inputs, weight_bf, preferred_element_type=jnp.float32) * inv_root
    gating = jax.nn.sigmoid(preact)
    derivative = gating * (1.0 + preact * (1.0 - gating))
    delta_rows = (upstream.astype(jnp.float32) * derivative * inv_root).astype(jnp.bfloat16)
    input_grad = jnp.dot(delta_rows, weight_bf.T, preferred_element_type=jnp.float32).astype(jnp.bfloat16)
    weight_grad = lax.dot_general(inputs, delta_rows, (((0,), (0,)), ((), ())), preferred_element_type=jnp.float32)
    new_first = 0.9 * first_moment + 0.1 * weight_grad
    new_second = 0.95 * second_moment + 0.05 * weight_grad * weight_grad
    steps = step_count[0].astype(jnp.float32)
    bias_one = 1.0 - jnp.power(jnp.float32(0.9), steps)
    bias_two = 1.0 - jnp.power(jnp.float32(0.95), steps)
    update = new_first / bias_one / (jnp.sqrt(new_second / bias_two) + 1e-08)
    inner = params - 0.1 * (update + 0.1 * params)
    return (inner, new_first, new_second, input_grad)

def reference(inputs, upstream, params, first_moment, second_moment, anchor, outer_moment, step_count):
    outer_grad = lax.optimization_barrier(jnp.sum(anchor[None] - params, axis=0)) / REPLICAS
    new_outer = 0.9 * outer_moment + outer_grad
    new_anchor = anchor - 0.7 * (outer_grad + 0.9 * new_outer)
    finals, firsts, seconds, grads = ([], [], [], [])
    for index in range(REPLICAS):
        inner, new_first, new_second, input_grad = one_replica(inputs[index], upstream[index], params[index], first_moment[index], second_moment[index], anchor, step_count, outer_grad)
        finals.append(0.5 * new_anchor + 0.5 * inner)
        firsts.append(new_first)
        seconds.append(new_second)
        grads.append(input_grad)
    return (jnp.stack(finals), jnp.stack(firsts), jnp.stack(seconds), new_anchor, new_outer, jnp.stack(grads))
```

```python
import math

import jax
import jax.numpy as jnp
from jax import lax
from jax.sharding import Mesh
from jax.sharding import PartitionSpec as P

Z = ("zh", "zl")
ZC = ("zh", "zl", "c")
SWAP = [(0, 1), (1, 0)]


def ring(step):
    return [(z, (z + step) % 16) for z in range(16)]


def ring_by_core(step):
    forward = [(2 * z, 2 * ((z + step) % 16)) for z in range(16)]
    backward = [(2 * z + 1, 2 * ((z - step) % 16) + 1) for z in range(16)]
    return forward + backward


def exchange(value, axes):
    return lax.all_to_all(value, axes, split_axis=0, concat_axis=0)


def gather_weight(own):
    same = exchange(jnp.broadcast_to(own[None], (4,) + own.shape), "zh")
    return [
        same,
        lax.ppermute(same, Z, ring(-1)),
        lax.ppermute(same, ZC, ring_by_core(2)),
        lax.ppermute(same, Z, ring(1)),
    ]


def scatter_grad(pieces):
    half = lambda value: value.astype(jnp.bfloat16)
    far = lax.ppermute(half(pieces[2]), ZC, ring_by_core(2))
    after = lax.ppermute(half(pieces[1]), Z, ring(1))
    before = lax.ppermute(half(pieces[3]), Z, ring(-1))
    wide = lambda value: value.astype(jnp.float32)
    summed = pieces[0] + wide(after) + wide(before) + wide(far)
    return jnp.sum(wide(exchange(half(summed), "zh")), axis=0)


def body(inputs, upstream, params, first_moment, second_moment, anchor, outer_moment, step_count):
    tokens_in = inputs[0]
    cotangent = upstream[0]
    master = params[0]
    rows, features = tokens_in.shape
    inv_root = 1.0 / math.sqrt(features)
    mine = lax.axis_index("y")
    turn = lax.axis_index("zl")

    summed = lax.psum(anchor - master, "replica")

    own = master.astype(jnp.bfloat16).reshape(64, 2, 256).transpose(1, 0, 2)
    own = exchange(own, "c").reshape(128, 256)
    weight = [piece.reshape(512, 256) for piece in gather_weight(own)]

    halves = tokens_in.reshape(rows, 2, 2048)
    kept = lax.dynamic_index_in_dim(halves, mine, 1, keepdims=False)
    given = lax.dynamic_index_in_dim(halves, 1 - mine, 1, keepdims=False)
    pair = jnp.stack([kept, lax.ppermute(given, "y", SWAP)])
    wide = lax.all_gather(pair, "c", axis=0).reshape(512, 4, 4, 128)
    wide = jnp.concatenate([wide, wide], axis=2)
    tokens = [
        lax.dynamic_slice_in_dim(wide, turn + k, 1, axis=2).reshape(512, 512) for k in range(4)
    ]
    both = jnp.stack([cotangent, lax.ppermute(cotangent, "y", SWAP)])
    both = both.reshape(2, rows, 2, 256).transpose(2, 0, 1, 3)
    both = exchange(both, "c").reshape(512, 256).astype(jnp.float32)

    partial = jnp.zeros((512, 256), jnp.float32)
    for k in range(4):
        partial += jnp.dot(tokens[k], weight[k], preferred_element_type=jnp.float32)
    other = lax.ppermute(partial, "y", SWAP).reshape(2, 2, rows, 256)
    other = jnp.flip(other, 1).reshape(512, 256)
    preact = (partial + other) * inv_root
    gating = jax.nn.sigmoid(preact)
    derivative = gating * (1.0 + preact * (1.0 - gating))
    delta = (both * derivative * inv_root).astype(jnp.bfloat16)

    contract = (((0,), (0,)), ((), ()))
    grads = [
        lax.dot_general(tokens[k], delta, contract, preferred_element_type=jnp.float32).reshape(
            4, 128, 256
        )
        for k in range(4)
    ]
    weight_grad = scatter_grad(grads)
    weight_grad = exchange(weight_grad.reshape(2, 64, 256), "c")
    weight_grad = weight_grad.transpose(1, 0, 2).reshape(64, 512)

    full = lax.all_gather(jnp.stack(weight), "c", axis=0)
    delta_own = exchange(delta.reshape(2, 256, 256), "c")
    back = [
        jnp.dot(delta_own[0], full[0, k].T, preferred_element_type=jnp.float32)
        + jnp.dot(delta_own[1], full[1, k].T, preferred_element_type=jnp.float32)
        for k in range(4)
    ]
    back = jnp.stack([b.astype(jnp.bfloat16).reshape(256, 4, 128) for b in back], axis=2)
    back = jnp.concatenate([back, back], axis=2)
    back = lax.dynamic_slice_in_dim(back, (4 - turn) % 4, 4, axis=2).reshape(2, rows, 2048)
    far = lax.ppermute(back[1], "y", SWAP)
    low = jnp.where(mine == 0, back[0], far)
    high = jnp.where(mine == 0, far, back[0])
    input_grad = jnp.concatenate([low, high], axis=1)

    new_first = 0.9 * first_moment[0] + 0.1 * weight_grad
    new_second = 0.95 * second_moment[0] + 0.05 * weight_grad * weight_grad
    steps = step_count[0].astype(jnp.float32)
    bias_one = 1.0 - jnp.power(jnp.float32(0.9), steps)
    bias_two = 1.0 - jnp.power(jnp.float32(0.95), steps)
    update = new_first / bias_one / (jnp.sqrt(new_second / bias_two) + 1e-08)
    inner = master - 0.1 * (update + 0.1 * master)
    outer_grad = summed / lax.axis_size("replica")
    new_outer = 0.9 * outer_moment + outer_grad
    new_anchor = anchor - 0.7 * (outer_grad + 0.9 * new_outer)
    new_params = 0.5 * new_anchor + 0.5 * inner
    return (
        new_params[None],
        new_first[None],
        new_second[None],
        new_anchor,
        new_outer,
        input_grad[None],
    )


def solution(mesh):
    replicas = mesh.shape["replica"]
    split = Mesh(mesh.devices.reshape(replicas, 2, 4, 4, 2), ("replica", "y", "zh", "zl", "c"))
    fsdp = ("y", "zh", "zl", "c")
    sharded = P("replica", fsdp, None)
    shared = P(fsdp, None)
    return jax.shard_map(
        body,
        mesh=split,
        in_specs=(sharded, sharded, sharded, sharded, sharded, shared, shared, P()),
        out_specs=(sharded, sharded, sharded, shared, shared, sharded),
        check_vma=False,
    )
```

```python
import math

import jax
import jax.numpy as jnp
from jax import lax
from jax.experimental import pallas as pl
from jax.experimental.pallas import tpu as pltpu
from jax.sharding import Mesh
from jax.sharding import PartitionSpec as P

Z = ("zh", "zl")
ZC = ("zh", "zl", "c")
SWAP = [(0, 1), (1, 0)]
BF16 = jnp.bfloat16
F32 = jnp.float32


def ring(step):
    return [(z, (z + step) % 16) for z in range(16)]


def ring_by_core(step):
    forward = [(2 * z, 2 * ((z + step) % 16)) for z in range(16)]
    backward = [(2 * z + 1, 2 * ((z - step) % 16) + 1) for z in range(16)]
    return forward + backward


def call(kernel, out_shape, flops, moved, operands, pinned=()):
    smem = pl.BlockSpec(memory_space=pltpu.SMEM)
    vmem = pl.BlockSpec(memory_space=pltpu.VMEM)
    hold = pl.BlockSpec(memory_space=pl.ANY)
    used = len(operands)

    def run(*refs):
        kernel(*refs[:used], *refs[used + len(pinned) :])

    return pl.pallas_call(
        run,
        out_shape=out_shape,
        in_specs=[smem] + [vmem] * (used - 1) + [hold] * len(pinned),
        out_specs=[vmem] * len(out_shape),
        compiler_params=pltpu.CompilerParams(vmem_limit_bytes=32 * 1024 * 1024),
        cost_estimate=pl.CostEstimate(flops=flops, bytes_accessed=moved, transcendentals=0),
    )(*operands, *pinned)


def shape(dims, dtype):
    return jax.ShapeDtypeStruct(dims, dtype)


def block(turn, k, high):
    return pl.multiple_of((high * 4 + lax.rem(turn + k, 4)) * 128, 128)


def weight_kernel(place, master, out):
    rounded = master[...].astype(BF16)
    for high in range(4):
        out[2 * high] = rounded[:, 0:256]
        out[2 * high + 1] = rounded[:, 256:512]


def give_kernel(place, x, cotangent, anchor, master, send, drift):
    drift[...] = anchor[...] - master[...]
    half = pl.multiple_of((1 - place[1]) * 2048, 2048)
    send[:, 0:2048] = x[:, pl.ds(half, 2048)]
    send[:, 2048:2560] = cotangent[...]


def share_kernel(place, x, got, cotangent, drift, send, kept):
    kept[...] = drift[...]
    half = pl.multiple_of(place[1] * 2048, 2048)
    keys = pl.multiple_of((1 - place[2]) * 256, 256)
    send[0:128, 0:2048] = x[:, pl.ds(half, 2048)]
    send[0:128, 2048:2304] = cotangent[:, pl.ds(keys, 256)]
    send[128:256, 0:2048] = got[:, 0:2048]
    send[128:256, 2048:2304] = got[:, pl.ds(pl.multiple_of(2048 + keys, 256), 256)]


def weight_kernel(place, master, out):
    rounded = master[...].astype(BF16)
    for high in range(4):
        out[2 * high] = rounded[:, 0:256]
        out[2 * high + 1] = rounded[:, 256:512]


def give_kernel(place, x, cotangent, anchor, master, send, drift):
    drift[...] = anchor[...] - master[...]
    half = pl.multiple_of((1 - place[1]) * 2048, 2048)
    send[:, 0:2048] = x[:, pl.ds(half, 2048)]
    send[:, 2048:2560] = cotangent[...]


def share_kernel(place, x, got, cotangent, drift, send, kept):
    kept[...] = drift[...]
    half = pl.multiple_of(place[1] * 2048, 2048)
    keys = pl.multiple_of((1 - place[2]) * 256, 256)
    send[0:128, 0:2048] = x[:, pl.ds(half, 2048)]
    send[0:128, 2048:2304] = cotangent[:, pl.ds(keys, 256)]
    send[128:256, 0:2048] = got[:, 0:2048]
    send[128:256, 2048:2304] = got[:, pl.ds(pl.multiple_of(2048 + keys, 256), 256)]


def order_kernel(place, x, got, near, cotangent, tokens, upstream):
    turn, mine, core = place[0], place[1], place[2]
    half = pl.multiple_of(mine * 2048, 2048)
    keys = pl.multiple_of(core * 256, 256)
    for k in range(4):
        for high in range(4):
            start = block(turn, k, high)
            to = pl.ds(high * 128, 128)
            tokens[k, 0:128, to] = x[:, pl.ds(pl.multiple_of(half + start, 128), 128)]
            tokens[k, 128:256, to] = got[:, pl.ds(start, 128)]
            tokens[k, 256:512, to] = near[:, pl.ds(start, 128)]
    upstream[0:128, :] = cotangent[:, pl.ds(keys, 256)]
    upstream[128:256, :] = got[:, pl.ds(pl.multiple_of(2048 + keys, 256), 256)]
    upstream[256:512, :] = near[:, 2048:2304]


def preact_own_kernel(place, x, got, w0, w1, w2, w3, partial, tokens):
    turn = place[0]
    half = pl.multiple_of(place[1] * 2048, 2048)
    total = jnp.zeros((256, 256), F32)
    for k, weight in enumerate((w0, w1, w2, w3)):
        for high in range(4):
            start = block(turn, k, high)
            to = pl.ds(high * 128, 128)
            tokens[k, 0:128, to] = x[:, pl.ds(pl.multiple_of(half + start, 128), 128)]
            tokens[k, 128:256, to] = got[:, pl.ds(start, 128)]
        total += jnp.dot(tokens[k], weight[...], preferred_element_type=F32)
    partial[...] = total


def preact_near_kernel(place, near, w0, w1, w2, w3, partial, tokens):
    turn = place[0]
    total = jnp.zeros((256, 256), F32)
    for k, weight in enumerate((w0, w1, w2, w3)):
        for high in range(4):
            to = pl.ds(high * 128, 128)
            tokens[k, :, to] = near[:, pl.ds(block(turn, k, high), 128)]
        total += jnp.dot(tokens[k], weight[...], preferred_element_type=F32)
    partial[...] = total


def turn_kernel(place, own, other, cotangent, got, near, w0, w1, w2, w3, turned, upstream, packed):
    keys = pl.multiple_of(place[2] * 256, 256)
    for k, weight in enumerate((w0, w1, w2, w3)):
        turned[k, :, 0:256] = own[k].T
        turned[k, :, 256:512] = other[k].T
        packed[k] = weight[...]
    upstream[0:128, :] = cotangent[:, pl.ds(keys, 256)]
    upstream[128:256, :] = got[:, pl.ds(pl.multiple_of(2048 + keys, 256), 256)]
    upstream[256:512, :] = near[:, 2048:2304]


def delta_kernel(inv_root, place, p0, p1, o0, o1, upstream, turned, delta, g0, g1, g2, g3):
    for row in range(0, 512, 128):
        here = slice(row, row + 128)
        mine = slice(row % 256, row % 256 + 128)
        theirs = slice((row ^ 128) % 256, (row ^ 128) % 256 + 128)
        partial, other = (p0, o0) if row < 256 else (p1, o1)
        preact = (partial[mine, :] + other[theirs, :]) * inv_root
        gating = jax.nn.sigmoid(preact)
        derivative = gating * (1.0 + preact * (1.0 - gating))
        rows = upstream[here, :].astype(F32) * derivative * inv_root
        delta[here, :] = rows.astype(BF16)
    for k, grad in ((2, g2), (1, g1), (3, g3), (0, g0)):
        full = jnp.dot(turned[k], delta[...], preferred_element_type=F32)
        grad[...] = full.astype(grad.dtype)


def back(delta, weight):
    return lax.dot_general(delta, weight, (((1,), (1,)), ((), ())), preferred_element_type=F32)


def back_kernel(place, delta, near, weight, near_weight, out, away):
    turn = place[0]
    for k in range(4):
        total = back(delta[0:256, :], weight[k]) + back(near[...], near_weight[k])
        total = total.astype(BF16)
        for high in range(4):
            to = pl.ds(block(turn, k, high), 128)
            out[:, to] = total[0:128, high * 128 : high * 128 + 128]
            away[:, to] = total[128:256, high * 128 : high * 128 + 128]


def total_kernel(place, g0, after, before, far, drift, total, kept):
    kept[...] = drift[...]
    summed = g0[...] + after[...].astype(F32) + before[...].astype(F32) + far[...].astype(F32)
    total[...] = summed.astype(BF16)


def body(inputs, upstream, params, first_moment, second_moment, anchor, outer_moment, step_count):
    tokens_in = inputs[0]
    cotangent = upstream[0]
    master = params[0]
    rows, features = tokens_in.shape
    inv_root = 1.0 / math.sqrt(features)
    mine = lax.axis_index("y")
    core = lax.axis_index("c")
    place = jnp.stack([lax.axis_index("zl"), mine, core]).astype(jnp.int32)

    (own,) = call(weight_kernel, [shape((8, 64, 256), BF16)], 0, 1 << 19, (place, master))
    same = lax.all_to_all(own, ("zh", "c"), split_axis=0, concat_axis=0).reshape(512, 256)
    weight = [
        same,
        lax.ppermute(same, Z, ring(-1)),
        lax.ppermute(same, ZC, ring_by_core(2)),
        lax.ppermute(same, Z, ring(1)),
    ]

    replicas = lax.axis_size("replica")

    def fold(value, flip):
        if flip >= replicas:
            return value
        pairs = [(r, r ^ flip) for r in range(replicas)]
        return value + lax.ppermute(value, "replica", pairs)

    given, drift = call(
        give_kernel,
        [shape((rows, 2560), BF16), shape((64, 512), F32)],
        0,
        1 << 20,
        (place, tokens_in, cotangent, anchor, master),
    )
    got = lax.ppermute(given, "y", SWAP)
    drift = fold(drift, 1)
    shared, drift = call(
        share_kernel,
        [shape((256, 2304), BF16), shape((64, 512), F32)],
        0,
        2 << 20,
        (place, tokens_in, got, cotangent, drift),
        weight[1:],
    )
    near = lax.ppermute(shared, "c", SWAP)

    partial_shapes = [shape((256, 256), F32), shape((4, 256, 512), BF16)]
    cost = 2 * 256 * 2048 * 256
    partial, tokens = call(
        preact_own_kernel, partial_shapes, cost, 3 << 20, (place, tokens_in, got, *weight)
    )
    other = lax.ppermute(partial, "y", SWAP)
    partial_near, tokens_near = call(
        preact_near_kernel, partial_shapes, cost, 3 << 20, (place, near, *weight)
    )
    other_near = lax.ppermute(partial_near, "y", SWAP)
    turned, both, packed = call(
        turn_kernel,
        [shape((4, 512, 512), BF16), shape((512, 256), BF16), shape((4, 512, 256), BF16)],
        0,
        4 << 20,
        (place, tokens, tokens_near, cotangent, got, near, *weight),
        (partial_near,),
    )
    near_weight = lax.ppermute(packed, "c", SWAP)
    drift = fold(drift, 3)
    delta, g0, g1, g2, g3 = call(
        lambda *refs: delta_kernel(inv_root, *refs),
        [shape((512, 256), BF16), shape((512, 256), F32)] + [shape((512, 256), BF16)] * 3,
        2 * 512 * 2048 * 256,
        5 << 20,
        (place, partial, partial_near, other, other_near, both, turned),
        (drift, near_weight),
    )

    far = lax.ppermute(g2, ZC, ring_by_core(2))
    after = lax.ppermute(g1, Z, ring(1))
    before = lax.ppermute(g3, Z, ring(-1))

    near_delta = lax.ppermute(delta[256:], "c", SWAP)
    stay, away = call(
        back_kernel,
        [shape((rows, 2048), BF16)] * 2,
        2 * 256 * 2048 * 512,
        4 << 20,
        (place, delta, near_delta, packed, near_weight),
        (after, before, far),
    )
    back_far = lax.ppermute(away, "y", SWAP)
    input_grad = jnp.concatenate(
        [jnp.where(mine == 0, stay, back_far), jnp.where(mine == 0, back_far, stay)], axis=1
    )

    total, drift = call(
        total_kernel,
        [shape((512, 256), BF16), shape((64, 512), F32)],
        0,
        2 << 20,
        (place, g0, after, before, far, drift),
        (away,),
    )
    parts = lax.all_to_all(total.reshape(8, 64, 256), ("zh", "c"), split_axis=0, concat_axis=0)
    weight_grad = jnp.sum(parts.reshape(4, 2, 64, 256).astype(F32), axis=0)
    weight_grad = weight_grad.transpose(1, 0, 2).reshape(64, 512)
    summed = fold(drift, 4)

    new_first = 0.9 * first_moment[0] + 0.1 * weight_grad
    new_second = 0.95 * second_moment[0] + 0.05 * weight_grad * weight_grad
    steps = step_count[0].astype(F32)
    bias_one = 1.0 - jnp.power(jnp.float32(0.9), steps)
    bias_two = 1.0 - jnp.power(jnp.float32(0.95), steps)
    update = new_first / bias_one / (jnp.sqrt(new_second / bias_two) + 1e-08)
    inner = master - 0.1 * (update + 0.1 * master)
    outer_grad = summed / replicas
    new_outer = 0.9 * outer_moment + outer_grad
    new_anchor = anchor - 0.7 * (outer_grad + 0.9 * new_outer)
    new_params = 0.5 * new_anchor + 0.5 * inner
    return (
        new_params[None],
        new_first[None],
        new_second[None],
        new_anchor,
        new_outer,
        input_grad[None],
    )


def solution(mesh):
    replicas = mesh.shape["replica"]
    split = Mesh(mesh.devices.reshape(replicas, 2, 4, 4, 2), ("replica", "y", "zh", "zl", "c"))
    fsdp = ("y", "zh", "zl", "c")
    sharded = P("replica", fsdp, None)
    shared = P(fsdp, None)
    return jax.shard_map(
        body,
        mesh=split,
        in_specs=(sharded, sharded, sharded, sharded, sharded, shared, shared, P()),
        out_specs=(sharded, sharded, sharded, shared, shared, sharded),
        check_vma=False,
    )
```

```python
import math

import jax
import jax.numpy as jnp
from jax import lax
from jax.experimental import pallas as pl
from jax.experimental.pallas import tpu as pltpu
from jax.sharding import Mesh
from jax.sharding import PartitionSpec as P

Z = ("zh", "zl")
ZC = ("zh", "zl", "c")
SWAP = [(0, 1), (1, 0)]
VMEM = 6 * 1024 * 1024
BESIDE = 20_000_000_000
BF16 = jnp.bfloat16
F32 = jnp.float32


def ring(step):
    return [(z, (z + step) % 16) for z in range(16)]


def ring_by_core(step):
    forward = [(2 * z, 2 * ((z + step) % 16)) for z in range(16)]
    backward = [(2 * z + 1, 2 * ((z - step) % 16) + 1) for z in range(16)]
    return forward + backward


def call(kernel, out_shape, flops, moved, operands, pinned=()):
    smem = pl.BlockSpec(memory_space=pltpu.SMEM)
    vmem = pl.BlockSpec(memory_space=pltpu.VMEM)
    hold = pl.BlockSpec(memory_space=pl.ANY)
    used = len(operands)

    def run(*refs):
        kernel(*refs[:used], *refs[used + len(pinned) :])

    return pl.pallas_call(
        run,
        out_shape=out_shape,
        in_specs=[smem] + [vmem] * (used - 1) + [hold] * len(pinned),
        out_specs=[vmem] * len(out_shape),
        compiler_params=pltpu.CompilerParams(vmem_limit_bytes=VMEM),
        cost_estimate=pl.CostEstimate(flops=flops, bytes_accessed=moved, transcendentals=0),
    )(*operands, *pinned)


def shape(dims, dtype):
    return jax.ShapeDtypeStruct(dims, dtype)


def block(turn, k, high):
    return pl.multiple_of((high * 4 + lax.rem(turn + k, 4)) * 128, 128)


def pack_kernel(place, w0, w1, w2, w3, packed):
    for k, weight in enumerate((w0, w1, w2, w3)):
        packed[k] = weight[...]


def preact_kernel(place, x, from_y, from_core, from_both, packed, anchor, master, partial, tokens, drift):
    drift[...] = anchor[...] - master[...]
    turn = place[0]
    half = pl.multiple_of(place[1] * 2048, 2048)
    total = jnp.zeros((512, 256), F32)
    for k in range(4):
        for high in range(4):
            start = block(turn, k, high)
            to = pl.ds(high * 128, 128)
            tokens[k, 0:128, to] = x[:, pl.ds(pl.multiple_of(half + start, 128), 128)]
            tokens[k, 128:256, to] = from_y[:, pl.ds(start, 128)]
            tokens[k, 256:384, to] = from_core[:, pl.ds(start, 128)]
            tokens[k, 384:512, to] = from_both[:, pl.ds(start, 128)]
        total += jnp.dot(tokens[k], packed[k], preferred_element_type=F32)
    for j in range(4):
        partial[:, j * 256 : j * 256 + 256] = total[j * 128 : j * 128 + 128, :]


def delta_kernel(
    inv_root, place, partial, other, cotangent, from_y, from_core, from_both, tokens, delta, g0, g1, g2, g3
):
    keys = pl.multiple_of(place[2] * 256, 256)
    upstream = (
        cotangent[:, pl.ds(keys, 256)],
        from_y[:, pl.ds(pl.multiple_of(2048 + keys, 256), 256)],
        from_core[:, 2048:2304],
        from_both[:, pl.ds(pl.multiple_of(2048 + keys, 256), 256)],
    )
    for j in range(4):
        i = j ^ 1
        preact = partial[:, j * 256 : j * 256 + 256] + other[:, i * 256 : i * 256 + 256]
        preact = preact * inv_root
        gating = jax.nn.sigmoid(preact)
        derivative = gating * (1.0 + preact * (1.0 - gating))
        rows = upstream[j].astype(F32) * derivative * inv_root
        delta[j * 128 : j * 128 + 128, :] = rows.astype(BF16)
    for k, grad in ((2, g2), (1, g1), (3, g3), (0, g0)):
        full = lax.dot_general(
            tokens[k], delta[...], (((0,), (0,)), ((), ())), preferred_element_type=F32
        )
        grad[...] = full.astype(grad.dtype)


def back(delta, weight):
    return lax.dot_general(delta, weight, (((1,), (1,)), ((), ())), preferred_element_type=F32)


def back_kernel(place, delta, near, weight, near_weight, out, away):
    turn = place[0]
    for k in range(4):
        total = back(delta[0:256, :], weight[k]) + back(near[...], near_weight[k])
        total = total.astype(BF16)
        for high in range(4):
            to = pl.ds(block(turn, k, high), 128)
            out[:, to] = total[0:128, high * 128 : high * 128 + 128]
            away[:, to] = total[128:256, high * 128 : high * 128 + 128]


def join_kernel(place, stay, far, out, sems):
    copies = []
    for source, y in ((stay, place[1]), (far, 1 - place[1])):
        to = out.at[:, pl.ds(pl.multiple_of(y * 2048, 2048), 2048)]
        copies.append(pltpu.make_async_copy(source, to, sems.at[len(copies)]))
    for copy in copies:
        copy.start()
    for copy in copies:
        copy.wait()


def total_kernel(place, g0, after, before, far, drift, total, kept):
    kept[...] = drift[...]
    summed = g0[...] + after[...].astype(F32) + before[...].astype(F32) + far[...].astype(F32)
    total[...] = summed.astype(BF16)


def sum_kernel(place, parts, out):
    for core in range(2):
        total = parts[core].astype(F32)
        for high in range(1, 4):
            total += parts[2 * high + core].astype(F32)
        out[:, core * 256 : core * 256 + 256] = total


def body(inputs, upstream, params, first_moment, second_moment, anchor, outer_moment, step_count):
    tokens_in = inputs[0]
    cotangent = upstream[0]
    master = params[0]
    rows, features = tokens_in.shape
    inv_root = 1.0 / math.sqrt(features)
    mine = lax.axis_index("y")
    core = lax.axis_index("c")
    place = jnp.stack([lax.axis_index("zl"), mine, core]).astype(jnp.int32)

    own = master.astype(BF16).reshape(64, 2, 256).transpose(1, 0, 2)
    own = jnp.broadcast_to(own[None], (4, 2, 64, 256)).reshape(8, 64, 256)
    same = lax.all_to_all(own, ("zh", "c"), split_axis=0, concat_axis=0).reshape(512, 256)
    weight = [
        same,
        lax.ppermute(same, Z, ring(-1)),
        lax.ppermute(same, ZC, ring_by_core(2)),
        lax.ppermute(same, Z, ring(1)),
    ]

    replicas = lax.axis_size("replica")

    def fold(value, flip):
        if flip >= replicas:
            return value
        pairs = [(r, r ^ flip) for r in range(replicas)]
        return value + lax.ppermute(value, "replica", pairs)

    def columns(y, keys):
        return jnp.concatenate(
            [lax.dynamic_slice_in_dim(tokens_in, y * 2048, 2048, axis=1), keys], axis=1
        )

    from_y = lax.ppermute(columns(1 - mine, cotangent), "y", SWAP)
    near_keys = jnp.where(core == 0, cotangent[:, 256:], cotangent[:, :256])
    from_core = lax.ppermute(columns(mine, near_keys), "c", SWAP)
    square = (from_y, from_core, lax.ppermute(from_y, "c", SWAP))

    (packed,) = call(
        pack_kernel, [shape((4, 512, 256), BF16)], BESIDE, 2 << 20, (place, *weight)
    )
    partial, tokens, drift = call(
        preact_kernel,
        [
            shape((rows, 1024), F32),
            shape((4, 512, 512), BF16),
            shape((64, 512), F32),
        ],
        2 * 512 * 2048 * 256,
        6 << 20,
        (place, tokens_in, *square, packed, anchor, master),
    )
    other = lax.ppermute(partial, "y", SWAP)
    drift = fold(drift, 1)
    near_weight = lax.ppermute(packed, "c", SWAP)
    delta, g0, g1, g2, g3 = call(
        lambda *refs: delta_kernel(inv_root, *refs),
        [shape((512, 256), BF16), shape((512, 256), F32)]
        + [shape((512, 256), BF16)] * 3,
        2 * 512 * 2048 * 256,
        5 << 20,
        (place, partial, other, cotangent, *square, tokens),
        (drift,),
    )
    far = lax.ppermute(g2, ZC, ring_by_core(2))
    after = lax.ppermute(g1, Z, ring(1))
    before = lax.ppermute(g3, Z, ring(-1))

    total, drift = call(
        total_kernel,
        [shape((512, 256), BF16), shape((64, 512), F32)],
        0,
        2 << 20,
        (place, g0, after, before, far, fold(drift, 3)),
    )
    parts = lax.all_to_all(total.reshape(8, 64, 256), ("zh", "c"), split_axis=0, concat_axis=0)
    (weight_grad,) = call(sum_kernel, [shape((64, 512), F32)], BESIDE, 1 << 19, (place, parts))
    summed = fold(drift, 4)

    near_delta = lax.ppermute(delta[256:], "c", SWAP)
    stay, away = call(
        back_kernel,
        [shape((rows, 2048), BF16)] * 2,
        2 * 256 * 2048 * 512,
        4 << 20,
        (place, delta, near_delta, packed, near_weight),
        (total,),
    )
    back_far = lax.ppermute(away, "y", SWAP)
    input_grad = jnp.concatenate(
        [jnp.where(mine == 0, stay, back_far), jnp.where(mine == 0, back_far, stay)], axis=1
    )

    new_first = 0.9 * first_moment[0] + 0.1 * weight_grad
    new_second = 0.95 * second_moment[0] + 0.05 * weight_grad * weight_grad
    steps = step_count[0].astype(F32)
    bias_one = 1.0 - jnp.power(jnp.float32(0.9), steps)
    bias_two = 1.0 - jnp.power(jnp.float32(0.95), steps)
    update = new_first / bias_one / (jnp.sqrt(new_second / bias_two) + 1e-08)
    inner = master - 0.1 * (update + 0.1 * master)
    outer_grad = summed / replicas
    new_outer = 0.9 * outer_moment + outer_grad
    new_anchor = anchor - 0.7 * (outer_grad + 0.9 * new_outer)
    new_params = 0.5 * new_anchor + 0.5 * inner
    return (
        new_params[None],
        new_first[None],
        new_second[None],
        new_anchor,
        new_outer,
        input_grad[None],
    )


def solution(mesh):
    replicas = mesh.shape["replica"]
    split = Mesh(mesh.devices.reshape(replicas, 2, 4, 4, 2), ("replica", "y", "zh", "zl", "c"))
    fsdp = ("y", "zh", "zl", "c")
    sharded = P("replica", fsdp, None)
    shared = P(fsdp, None)
    return jax.shard_map(
        body,
        mesh=split,
        in_specs=(sharded, sharded, sharded, sharded, sharded, shared, shared, P()),
        out_specs=(sharded, sharded, sharded, shared, shared, sharded),
        check_vma=False,
    )
```

```python
import math

import jax
import jax.numpy as jnp
from jax import lax
from jax.experimental import pallas as pl
from jax.experimental.pallas import tpu as pltpu
from jax.sharding import Mesh
from jax.sharding import PartitionSpec as P

Z = ("zh", "zl")
ZC = ("zh", "zl", "c")
SWAP = [(0, 1), (1, 0)]
VMEM = 6 * 1024 * 1024
BESIDE = 20_000_000_000
BF16 = jnp.bfloat16
F32 = jnp.float32


def ring(step):
    return [(z, (z + step) % 16) for z in range(16)]


def ring_by_core(step):
    forward = [(2 * z, 2 * ((z + step) % 16)) for z in range(16)]
    backward = [(2 * z + 1, 2 * ((z - step) % 16) + 1) for z in range(16)]
    return forward + backward


def call(kernel, out_shape, flops, moved, operands, pinned=()):
    smem = pl.BlockSpec(memory_space=pltpu.SMEM)
    vmem = pl.BlockSpec(memory_space=pltpu.VMEM)
    hold = pl.BlockSpec(memory_space=pl.ANY)
    used = len(operands)

    def run(*refs):
        kernel(*refs[:used], *refs[used + len(pinned) :])

    return pl.pallas_call(
        run,
        out_shape=out_shape,
        in_specs=[smem] + [vmem] * (used - 1) + [hold] * len(pinned),
        out_specs=[vmem] * len(out_shape),
        compiler_params=pltpu.CompilerParams(vmem_limit_bytes=VMEM),
        cost_estimate=pl.CostEstimate(flops=flops, bytes_accessed=moved, transcendentals=0),
    )(*operands, *pinned)


def shape(dims, dtype):
    return jax.ShapeDtypeStruct(dims, dtype)


def block(turn, k, high):
    return pl.multiple_of((high * 4 + lax.rem(turn + k, 4)) * 128, 128)


def pack_kernel(place, w0, w2, w1, w3, packed):
    for k, weight in enumerate((w0, w1, w2, w3)):
        packed[k] = weight[...]


def preact_kernel(place, x, from_y, from_core, from_both, packed, cotangent, anchor, master, partial, tokens, upstream, drift):
    drift[...] = anchor[...] - master[...]
    turn = place[0]
    half = pl.multiple_of(place[1] * 2048, 2048)
    total = jnp.zeros((512, 256), F32)
    for k in range(4):
        for high in range(4):
            start = block(turn, k, high)
            to = pl.ds(high * 128, 128)
            tokens[k, 0:128, to] = x[:, pl.ds(pl.multiple_of(half + start, 128), 128)]
            tokens[k, 128:256, to] = from_y[:, pl.ds(start, 128)]
            tokens[k, 256:384, to] = from_core[:, pl.ds(start, 128)]
            tokens[k, 384:512, to] = from_both[:, pl.ds(start, 128)]
        total += jnp.dot(tokens[k], packed[k], preferred_element_type=F32)
    keys = pl.multiple_of(place[2] * 256, 256)
    far_keys = pl.multiple_of(2048 + place[2] * 256, 256)
    upstream[0:128, :] = cotangent[:, pl.ds(keys, 256)]
    upstream[128:256, :] = from_y[:, pl.ds(far_keys, 256)]
    upstream[256:384, :] = from_core[:, 2048:2304]
    upstream[384:512, :] = from_both[:, pl.ds(far_keys, 256)]
    for j in range(4):
        partial[:, j * 256 : j * 256 + 256] = total[j * 128 : j * 128 + 128, :]


def delta_kernel(inv_root, place, partial, other, upstream, tokens, delta, g0, g1, g2, g3):
    for j in range(4):
        i = j ^ 1
        preact = partial[:, j * 256 : j * 256 + 256] + other[:, i * 256 : i * 256 + 256]
        preact = preact * inv_root
        gating = jax.nn.sigmoid(preact)
        derivative = gating * (1.0 + preact * (1.0 - gating))
        rows = upstream[j * 128 : j * 128 + 128, :].astype(F32) * derivative * inv_root
        delta[j * 128 : j * 128 + 128, :] = rows.astype(BF16)
    for k, grad in ((2, g2), (1, g1), (3, g3), (0, g0)):
        full = lax.dot_general(
            tokens[k], delta[...], (((0,), (0,)), ((), ())), preferred_element_type=F32
        )
        grad[...] = full.astype(grad.dtype)


def back(delta, weight):
    return lax.dot_general(delta, weight, (((1,), (1,)), ((), ())), preferred_element_type=F32)


def back_kernel(place, delta, near, weight, near_weight, out, away):
    turn = place[0]
    for k in range(4):
        total = back(delta[0:256, :], weight[k]) + back(near[...], near_weight[k])
        total = total.astype(BF16)
        for high in range(4):
            to = pl.ds(block(turn, k, high), 128)
            out[:, to] = total[0:128, high * 128 : high * 128 + 128]
            away[:, to] = total[128:256, high * 128 : high * 128 + 128]


def join_kernel(place, stay, far, out):
    out[:, pl.ds(pl.multiple_of(place[1] * 2048, 2048), 2048)] = stay[...]
    out[:, pl.ds(pl.multiple_of((1 - place[1]) * 2048, 2048), 2048)] = far[...]


def total_kernel(place, g0, far, after, before, drift, total, kept):
    kept[...] = drift[...]
    summed = g0[...] + after[...].astype(F32) + before[...].astype(F32) + far[...].astype(F32)
    total[...] = summed.astype(BF16)


def sum_kernel(place, parts, out):
    for core in range(2):
        total = parts[core].astype(F32)
        for high in range(1, 4):
            total += parts[2 * high + core].astype(F32)
        out[:, core * 256 : core * 256 + 256] = total


def body(inputs, upstream, params, first_moment, second_moment, anchor, outer_moment, step_count):
    tokens_in = inputs[0]
    cotangent = upstream[0]
    master = params[0]
    rows, features = tokens_in.shape
    inv_root = 1.0 / math.sqrt(features)
    mine = lax.axis_index("y")
    core = lax.axis_index("c")
    place = jnp.stack([lax.axis_index("zl"), mine, core]).astype(jnp.int32)

    own = master.astype(BF16).reshape(64, 2, 256).transpose(1, 0, 2)
    own = jnp.broadcast_to(own[None], (4, 2, 64, 256)).reshape(8, 64, 256)
    same = lax.all_to_all(own, ("zh", "c"), split_axis=0, concat_axis=0).reshape(512, 256)
    weight = [
        same,
        lax.ppermute(same, Z, ring(-1)),
        lax.ppermute(same, ZC, ring_by_core(2)),
        lax.ppermute(same, Z, ring(1)),
    ]

    replicas = lax.axis_size("replica")

    def fold(value, flip):
        if flip >= replicas:
            return value
        pairs = [(r, r ^ flip) for r in range(replicas)]
        return value + lax.ppermute(value, "replica", pairs)

    def columns(y, keys):
        return jnp.concatenate(
            [lax.dynamic_slice_in_dim(tokens_in, y * 2048, 2048, axis=1), keys], axis=1
        )

    from_y = lax.ppermute(columns(1 - mine, cotangent), "y", SWAP)
    near_keys = jnp.where(core == 0, cotangent[:, 256:], cotangent[:, :256])
    from_core = lax.ppermute(columns(mine, near_keys), "c", SWAP)
    square = (from_y, from_core, lax.ppermute(from_y, "c", SWAP))

    (packed,) = call(
        pack_kernel, [shape((4, 512, 256), BF16)], 10 * BESIDE, 2 << 20, (place, weight[0], weight[2], weight[1], weight[3])
    )
    partial, tokens, both, drift = call(
        preact_kernel,
        [
            shape((rows, 1024), F32),
            shape((4, 512, 512), BF16),
            shape((512, 256), BF16),
            shape((64, 512), F32),
        ],
        2 * 512 * 2048 * 256,
        6 << 20,
        (place, tokens_in, *square, packed, cotangent, anchor, master),
    )
    other = lax.ppermute(partial, "y", SWAP)
    drift = fold(drift, 1)
    near_weight = lax.ppermute(packed, "c", SWAP)
    delta, g0, g1, g2, g3 = call(
        lambda *refs: delta_kernel(inv_root, *refs),
        [shape((512, 256), BF16), shape((512, 256), F32)]
        + [shape((512, 256), BF16)] * 3,
        2 * 512 * 2048 * 256,
        5 << 20,
        (place, partial, other, both, tokens),
        (drift,),
    )
    far = lax.ppermute(g2, ZC, ring_by_core(2))
    after = lax.ppermute(g1, Z, ring(1))
    before = lax.ppermute(g3, Z, ring(-1))

    near_delta = lax.ppermute(delta[256:], "c", SWAP)
    total, drift = call(
        total_kernel,
        [shape((512, 256), BF16), shape((64, 512), F32)],
        0,
        2 << 20,
        (place, g0, far, after, before, fold(drift, 4)),
        (near_delta,),
    )
    parts = lax.all_to_all(total.reshape(8, 64, 256), ("zh", "c"), split_axis=0, concat_axis=0)
    (weight_grad,) = call(sum_kernel, [shape((64, 512), F32)], BESIDE, 1 << 19, (place, parts))
    summed = fold(drift, 3)

    stay, away = call(
        back_kernel,
        [shape((rows, 2048), BF16)] * 2,
        2 * 256 * 2048 * 512,
        4 << 20,
        (place, delta, near_delta, packed, near_weight),
        (total,),
    )
    back_far = lax.ppermute(away, "y", SWAP)
    (input_grad,) = call(
        join_kernel, [shape((rows, features), BF16)], 0, 2 << 20, (place, stay, back_far)
    )

    new_first = 0.9 * first_moment[0] + 0.1 * weight_grad
    new_second = 0.95 * second_moment[0] + 0.05 * weight_grad * weight_grad
    steps = step_count[0].astype(F32)
    bias_one = 1.0 - jnp.power(jnp.float32(0.9), steps)
    bias_two = 1.0 - jnp.power(jnp.float32(0.95), steps)
    update = new_first / bias_one / (jnp.sqrt(new_second / bias_two) + 1e-08)
    inner = master - 0.1 * (update + 0.1 * master)
    outer_grad = summed / replicas
    new_outer = 0.9 * outer_moment + outer_grad
    new_anchor = anchor - 0.7 * (outer_grad + 0.9 * new_outer)
    new_params = 0.5 * new_anchor + 0.5 * inner
    return (
        new_params[None],
        new_first[None],
        new_second[None],
        new_anchor,
        new_outer,
        input_grad[None],
    )


def solution(mesh):
    replicas = mesh.shape["replica"]
    split = Mesh(mesh.devices.reshape(replicas, 2, 4, 4, 2), ("replica", "y", "zh", "zl", "c"))
    fsdp = ("y", "zh", "zl", "c")
    sharded = P("replica", fsdp, None)
    shared = P(fsdp, None)
    return jax.shard_map(
        body,
        mesh=split,
        in_specs=(sharded, sharded, sharded, sharded, sharded, shared, shared, P()),
        out_specs=(sharded, sharded, sharded, shared, shared, sharded),
        check_vma=False,
    )
```

```python
import math

import jax
import jax.numpy as jnp
from jax import lax
from jax.experimental import pallas as pl
from jax.experimental.pallas import tpu as pltpu
from jax.sharding import Mesh
from jax.sharding import PartitionSpec as P

Z = ("zh", "zl")
ZC = ("zh", "zl", "c")
SWAP = [(0, 1), (1, 0)]
VMEM = 6 * 1024 * 1024
BESIDE = 20_000_000_000
BF16 = jnp.bfloat16
F32 = jnp.float32


def ring(step):
    return [(z, (z + step) % 16) for z in range(16)]


def ring_by_core(step):
    forward = [(2 * z, 2 * ((z + step) % 16)) for z in range(16)]
    backward = [(2 * z + 1, 2 * ((z - step) % 16) + 1) for z in range(16)]
    return forward + backward


def call(kernel, out_shape, flops, moved, operands, pinned=()):
    smem = pl.BlockSpec(memory_space=pltpu.SMEM)
    vmem = pl.BlockSpec(memory_space=pltpu.VMEM)
    hold = pl.BlockSpec(memory_space=pl.ANY)
    used = len(operands)

    def run(*refs):
        kernel(*refs[:used], *refs[used + len(pinned) :])

    return pl.pallas_call(
        run,
        out_shape=out_shape,
        in_specs=[smem] + [vmem] * (used - 1) + [hold] * len(pinned),
        out_specs=[vmem] * len(out_shape),
        compiler_params=pltpu.CompilerParams(vmem_limit_bytes=VMEM),
        cost_estimate=pl.CostEstimate(flops=flops, bytes_accessed=moved, transcendentals=0),
    )(*operands, *pinned)


def shape(dims, dtype):
    return jax.ShapeDtypeStruct(dims, dtype)


def block(turn, k, high):
    return pl.multiple_of((high * 4 + lax.rem(turn + k, 4)) * 128, 128)


def pack_kernel(place, w0, w2, w3, w1, packed):
    for k, weight in enumerate((w0, w1, w2, w3)):
        packed[k] = weight[...]


def preact_kernel(place, x, from_y, from_core, from_both, packed, cotangent, anchor, master, partial, tokens, upstream, drift):
    drift[...] = anchor[...] - master[...]
    turn = place[0]
    half = pl.multiple_of(place[1] * 2048, 2048)
    total = jnp.zeros((512, 256), F32)
    for k in range(4):
        for high in range(4):
            start = block(turn, k, high)
            to = pl.ds(high * 128, 128)
            tokens[k, 0:128, to] = x[:, pl.ds(pl.multiple_of(half + start, 128), 128)]
            tokens[k, 128:256, to] = from_y[:, pl.ds(start, 128)]
            tokens[k, 256:384, to] = from_core[:, pl.ds(start, 128)]
            tokens[k, 384:512, to] = from_both[:, pl.ds(start, 128)]
        total += jnp.dot(tokens[k], packed[k], preferred_element_type=F32)
    keys = pl.multiple_of(place[2] * 256, 256)
    far_keys = pl.multiple_of(2048 + place[2] * 256, 256)
    upstream[0:128, :] = cotangent[:, pl.ds(keys, 256)]
    upstream[128:256, :] = from_y[:, pl.ds(far_keys, 256)]
    upstream[256:384, :] = from_core[:, 2048:2304]
    upstream[384:512, :] = from_both[:, pl.ds(far_keys, 256)]
    for j in range(4):
        partial[:, j * 256 : j * 256 + 256] = total[j * 128 : j * 128 + 128, :]


def delta_kernel(inv_root, place, partial, other, upstream, tokens, delta, g0, g1, g2, g3):
    for j in range(4):
        i = j ^ 1
        preact = partial[:, j * 256 : j * 256 + 256] + other[:, i * 256 : i * 256 + 256]
        preact = preact * inv_root
        gating = jax.nn.sigmoid(preact)
        derivative = gating * (1.0 + preact * (1.0 - gating))
        rows = upstream[j * 128 : j * 128 + 128, :].astype(F32) * derivative * inv_root
        delta[j * 128 : j * 128 + 128, :] = rows.astype(BF16)
    for k, grad in ((2, g2), (1, g1), (3, g3), (0, g0)):
        full = lax.dot_general(
            tokens[k], delta[...], (((0,), (0,)), ((), ())), preferred_element_type=F32
        )
        grad[...] = full.astype(grad.dtype)


def back(delta, weight):
    return lax.dot_general(delta, weight, (((1,), (1,)), ((), ())), preferred_element_type=F32)


def back_kernel(place, delta, near, weight, near_weight, out, away):
    turn = place[0]
    for k in range(4):
        total = back(delta[0:256, :], weight[k]) + back(near[...], near_weight[k])
        total = total.astype(BF16)
        for high in range(4):
            to = pl.ds(block(turn, k, high), 128)
            out[:, to] = total[0:128, high * 128 : high * 128 + 128]
            away[:, to] = total[128:256, high * 128 : high * 128 + 128]


def join_kernel(place, stay, far, out):
    out[:, pl.ds(pl.multiple_of(place[1] * 2048, 2048), 2048)] = stay[...]
    out[:, pl.ds(pl.multiple_of((1 - place[1]) * 2048, 2048), 2048)] = far[...]


def total_kernel(place, g0, far, before, after, drift, total, kept):
    kept[...] = drift[...]
    summed = g0[...] + after[...].astype(F32) + before[...].astype(F32) + far[...].astype(F32)
    total[...] = summed.astype(BF16)


def sum_kernel(place, parts, out):
    for core in range(2):
        total = parts[core].astype(F32)
        for high in range(1, 4):
            total += parts[2 * high + core].astype(F32)
        out[:, core * 256 : core * 256 + 256] = total


def body(inputs, upstream, params, first_moment, second_moment, anchor, outer_moment, step_count):
    tokens_in = inputs[0]
    cotangent = upstream[0]
    master = params[0]
    rows, features = tokens_in.shape
    inv_root = 1.0 / math.sqrt(features)
    mine = lax.axis_index("y")
    core = lax.axis_index("c")
    place = jnp.stack([lax.axis_index("zl"), mine, core]).astype(jnp.int32)

    own = master.astype(BF16).reshape(64, 2, 256).transpose(1, 0, 2)
    own = jnp.broadcast_to(own[None], (4, 2, 64, 256)).reshape(8, 64, 256)
    same = lax.all_to_all(own, ("zh", "c"), split_axis=0, concat_axis=0).reshape(512, 256)
    weight = [
        same,
        lax.ppermute(same, Z, ring(-1)),
        lax.ppermute(same, ZC, ring_by_core(2)),
        lax.ppermute(same, Z, ring(1)),
    ]

    replicas = lax.axis_size("replica")

    def fold(value, flip):
        if flip >= replicas:
            return value
        pairs = [(r, r ^ flip) for r in range(replicas)]
        return value + lax.ppermute(value, "replica", pairs)

    def columns(y, keys):
        return jnp.concatenate(
            [lax.dynamic_slice_in_dim(tokens_in, y * 2048, 2048, axis=1), keys], axis=1
        )

    from_y = lax.ppermute(columns(1 - mine, cotangent), "y", SWAP)
    near_keys = jnp.where(core == 0, cotangent[:, 256:], cotangent[:, :256])
    from_core = lax.ppermute(columns(mine, near_keys), "c", SWAP)
    square = (from_y, from_core, lax.ppermute(from_y, "c", SWAP))

    (packed,) = call(
        pack_kernel, [shape((4, 512, 256), BF16)], 10 * BESIDE, 2 << 20, (place, weight[0], weight[2], weight[3], weight[1])
    )
    partial, tokens, both, drift = call(
        preact_kernel,
        [
            shape((rows, 1024), F32),
            shape((4, 512, 512), BF16),
            shape((512, 256), BF16),
            shape((64, 512), F32),
        ],
        2 * 512 * 2048 * 256,
        6 << 20,
        (place, tokens_in, *square, packed, cotangent, anchor, master),
    )
    other = lax.ppermute(partial, "y", SWAP)
    drift = fold(drift, 1)
    near_weight = lax.ppermute(packed, "c", SWAP)
    delta, g0, g1, g2, g3 = call(
        lambda *refs: delta_kernel(inv_root, *refs),
        [shape((512, 256), BF16), shape((512, 256), F32)]
        + [shape((512, 256), BF16)] * 3,
        2 * 512 * 2048 * 256,
        5 << 20,
        (place, partial, other, both, tokens),
        (drift,),
    )
    far = lax.ppermute(g2, ZC, ring_by_core(2))
    after = lax.ppermute(g1, Z, ring(1))
    before = lax.ppermute(g3, Z, ring(-1))

    near_delta = lax.ppermute(delta[256:], "c", SWAP)
    total, drift = call(
        total_kernel,
        [shape((512, 256), BF16), shape((64, 512), F32)],
        0,
        2 << 20,
        (place, g0, far, before, after, fold(drift, 4)),
        (near_delta,),
    )
    parts = lax.all_to_all(total.reshape(8, 64, 256), ("zh", "c"), split_axis=0, concat_axis=0)
    (weight_grad,) = call(sum_kernel, [shape((64, 512), F32)], BESIDE, 1 << 19, (place, parts))
    summed = fold(drift, 3)

    stay, away = call(
        back_kernel,
        [shape((rows, 2048), BF16)] * 2,
        2 * 256 * 2048 * 512,
        4 << 20,
        (place, delta, near_delta, packed, near_weight),
        (total,),
    )
    back_far = lax.ppermute(away, "y", SWAP)
    (input_grad,) = call(
        join_kernel, [shape((rows, features), BF16)], 0, 2 << 20, (place, stay, back_far)
    )

    new_first = 0.9 * first_moment[0] + 0.1 * weight_grad
    new_second = 0.95 * second_moment[0] + 0.05 * weight_grad * weight_grad
    steps = step_count[0].astype(F32)
    bias_one = 1.0 - jnp.power(jnp.float32(0.9), steps)
    bias_two = 1.0 - jnp.power(jnp.float32(0.95), steps)
    update = new_first / bias_one / (jnp.sqrt(new_second / bias_two) + 1e-08)
    inner = master - 0.1 * (update + 0.1 * master)
    outer_grad = summed / replicas
    new_outer = 0.9 * outer_moment + outer_grad
    new_anchor = anchor - 0.7 * (outer_grad + 0.9 * new_outer)
    new_params = 0.5 * new_anchor + 0.5 * inner
    return (
        new_params[None],
        new_first[None],
        new_second[None],
        new_anchor,
        new_outer,
        input_grad[None],
    )


def solution(mesh):
    replicas = mesh.shape["replica"]
    split = Mesh(mesh.devices.reshape(replicas, 2, 4, 4, 2), ("replica", "y", "zh", "zl", "c"))
    fsdp = ("y", "zh", "zl", "c")
    sharded = P("replica", fsdp, None)
    shared = P(fsdp, None)
    return jax.shard_map(
        body,
        mesh=split,
        in_specs=(sharded, sharded, sharded, sharded, sharded, shared, shared, P()),
        out_specs=(sharded, sharded, sharded, shared, shared, sharded),
        check_vma=False,
    )
```
